32 devices in a mesh: group: 2 (over y), tm: 4 (over z), seq: 2 (over x), mp: 2 (over core).
Axes of the slice: x: 2, y: 2, z: 4, core: 2. Of those that a mesh axis runs over, the one named last changes fastest.
Arguments:
- states: bfloat16 [8, 128, 5120], P(('group', 'tm'), 'seq'), parts along dimension 0, may hold values from -6 to 6
- start_step: int32 [2], P('group'), parts along dimension 0, may hold values from 0 to 96
- w_qkv: bfloat16 [3, 5120, 3072], P(None, 'tm', ('seq', 'mp')), may hold values from -0.078125 to 0.078125
- qk_gain: float32 [2, 3072], P(None, ('seq', 'mp')), may hold values from 0.25 to 1.75
- w_out: bfloat16 [5120, 3072], P('tm', ('seq', 'mp')), may hold values from -0.109375 to 0.109375
- time_proj: bfloat16 [256, 15360], P('tm'), may hold values from -0.375 to 0.375
Outputs:
- displacement: float32 [8, 128, 5120], P(('group', 'tm'), 'seq', 'mp'), parts along dimension 0
The draws below stay inside these ranges and needn't reach their ends.
There are 2 independent parts, one for each index of `group`. The reference program is written for one: setup_inputs(seed, part) draws one part's arguments, and reference() takes and returns one part's arrays. A program takes and returns all parts, laid end to end along the dimension named above; an argument that names none is the same for every part. Nothing has to cross between parts.
Inputs may be any that keep to these rules, and one draw needn't show every extreme that they name: `start_step`: the window lies inside the trajectory.
All inputs are finite; a program needn't handle non-finite values.
Results may differ from the reference program's by a relative error of at most 0.0029.
Values may be sent and summed in bfloat16 or wider, within the bound.
A program may use at most 128 MiB of HBM per device.

```python
import jax
import jax.numpy as jnp
from jax import lax

D = 5120
HEADS = 24
HEAD_DIM = 128
FREQ = 256
STEPS = 100
W = 4
L = 128


def steps_of(stream_key, extent, pieces, smallest, high):
    loudness, own = 1.0, jax.random.fold_in(stream_key, 6)
    for position, parts in pieces:
        steps = jnp.exp(jax.random.uniform(jax.random.fold_in(own, position), (parts,), jnp.float32, smallest / len(pieces), high / len(pieces)))
        loudness = loudness * jnp.repeat(steps, extent[position] // parts).reshape([-1 if axis == position else 1 for axis in range(len(extent))])
    return loudness


def noise(rng, dims, deviation, reach, split=(), kind=jnp.bfloat16):
    loudness = steps_of(rng, dims, split, -0.22, 0.18) if split else 1.0
    result = jax.random.normal(rng, dims, jnp.float32) * deviation * loudness
    return jnp.minimum(jnp.maximum(result, -reach), reach).astype(kind)


def setup_inputs(seed: int = 0, part: int = 0) -> dict:
    key_list = jax.random.split(jax.random.key(seed), 7)
    own_keys = jax.random.split(jax.random.fold_in(key_list[6], part), 7)
    return {
        "states": noise(own_keys[0], (W, L, D), 1.0, 6.0, ((0, 4), (1, 2))),
        "start_step": jax.random.randint(own_keys[1], (1,), 0, STEPS - W + 1).astype(jnp.int32),
        "w_qkv": noise(key_list[2], (3, D, HEADS * HEAD_DIM), D ** -0.5, 0.078125, ((1, 4), (2, 4))),
        "qk_gain": jnp.clip(1.0 + 0.15 * jax.random.normal(key_list[3], (2, HEADS * HEAD_DIM), jnp.float32), 0.25, 1.75),
        "w_out": noise(key_list[4], (D, HEADS * HEAD_DIM), (HEADS * HEAD_DIM) ** -0.5, 0.109375, ((0, 4), (1, 4))),
        "time_proj": noise(key_list[5], (FREQ, 3 * D), FREQ ** -0.5, 0.375, ((0, 4),)),
    }


sample_shift = 5.0
norm_eps = 1e-06

def sigma_of(index):
    unit = 1.0 - index.astype(jnp.float32) / jnp.float32(STEPS)
    return sample_shift * unit / (1.0 + (sample_shift - 1.0) * unit)

def embed_time(sigma_now):
    half_freq = FREQ // 2
    ranks = jnp.arange(half_freq).astype(jnp.float32)
    freqs = jnp.exp(-jnp.log(jnp.float32(10000.0)) * ranks / jnp.float32(half_freq))
    angles = (1000.0 * sigma_now)[:, None] * freqs[None, :]
    return jnp.concatenate([jnp.cos(angles), jnp.sin(angles)], axis=1).astype(jnp.bfloat16)

def head_norm(values, gain):
    shaped = values.reshape(W, L, HEADS, HEAD_DIM)
    meansq = lax.optimization_barrier(jnp.mean(shaped * shaped, axis=-1, keepdims=True))
    scaled = shaped * lax.rsqrt(meansq + norm_eps) * gain.reshape(HEADS, HEAD_DIM)
    return scaled.astype(jnp.bfloat16)

def reference(states, start_step, w_qkv, qk_gain, w_out, time_proj):
    steps_idx = start_step[0].astype(jnp.int32) + jnp.arange(W).astype(jnp.int32)
    sigma_now = sigma_of(steps_idx)
    step_size = sigma_of(steps_idx + 1) - sigma_now
    emb = embed_time(sigma_now)
    modulation = jnp.dot(emb, time_proj, preferred_element_type=jnp.float32)
    shift = modulation[:, :D]
    scale = modulation[:, D:2 * D]
    gate = modulation[:, 2 * D:]
    field = states.astype(jnp.float32)
    mean = lax.optimization_barrier(jnp.mean(field, axis=-1, keepdims=True))
    centred = field - mean
    var = lax.optimization_barrier(jnp.mean(centred * centred, axis=-1, keepdims=True))
    normed = centred * lax.rsqrt(var + norm_eps)
    hidden = (normed * (1.0 + scale[:, None, :]) + shift[:, None, :]).astype(jnp.bfloat16)
    flat = hidden.reshape(W * L, D)
    query = head_norm(jnp.dot(flat, w_qkv[0], preferred_element_type=jnp.float32), qk_gain[0])
    keys = head_norm(jnp.dot(flat, w_qkv[1], preferred_element_type=jnp.float32), qk_gain[1])
    values = jnp.dot(flat, w_qkv[2], preferred_element_type=jnp.float32).astype(jnp.bfloat16).reshape(W, L, HEADS, HEAD_DIM)
    inv_root = 1.0 / jnp.sqrt(jnp.float32(HEAD_DIM))

    def one_head(operands):
        q_head, k_head, v_head = operands
        scores = jnp.einsum('wqd,wkd->wqk', q_head.astype(jnp.float32), k_head.astype(jnp.float32)) * inv_root
        expo = jnp.exp(scores)
        probs = (expo / lax.optimization_barrier(jnp.sum(expo, axis=-1, keepdims=True))).astype(jnp.bfloat16)
        return jnp.einsum('wqk,wkd->wqd', probs.astype(jnp.float32), v_head.astype(jnp.float32)).astype(jnp.bfloat16)
    heads_out = lax.map(one_head, (jnp.moveaxis(query, 2, 0), jnp.moveaxis(keys, 2, 0), jnp.moveaxis(values, 2, 0)))
    attn = jnp.moveaxis(heads_out, 0, 2).reshape(W * L, HEADS * HEAD_DIM)
    out = jnp.dot(attn, w_out.T, preferred_element_type=jnp.float32).reshape(W, L, D)
    drift = gate[:, None, :] * out
    increments = step_size[:, None, None] * drift
    return jnp.cumsum(increments, axis=0)
```

```python
import functools

import jax
import jax.numpy as jnp
from jax import lax
from jax.experimental import pallas as pl
from jax.experimental.pallas import tpu as pltpu
from jax.sharding import PartitionSpec as P

HEAD_DIM = 128
FREQ = 256
STEPS = 100

sample_shift = 5.0
norm_eps = 1e-06

MESH = pl.DeviceIdType.MESH
F32 = jnp.float32
BF16 = jnp.bfloat16


def sigma_of(index):
    unit = 1.0 - index.astype(jnp.float32) / jnp.float32(STEPS)
    return sample_shift * unit / (1.0 + (sample_shift - 1.0) * unit)


def embed_time(sigma_now):
    half_freq = FREQ // 2
    ranks = jnp.arange(half_freq).astype(jnp.float32)
    freqs = jnp.exp(-jnp.log(jnp.float32(10000.0)) * ranks / jnp.float32(half_freq))
    angles = (1000.0 * sigma_now)[:, None] * freqs[None, :]
    return jnp.concatenate([jnp.cos(angles), jnp.sin(angles)], axis=1).astype(jnp.bfloat16)


def remote(src, dst, send_sem, recv_sem, **where):
    return pltpu.make_async_remote_copy(
        src_ref=src, dst_ref=dst, send_sem=send_sem, recv_sem=recv_sem,
        device_id=where, device_id_type=MESH,
    )


def sweep_kernel(
    cfg, xb, modp, dtb, gains, w_qkv, w_out, out,
    xin, st_out, st_in, mod_in, mods, hid, wq, wo, own, chain, probs_ref, at, run, pp, sib, xo, xi, zo, zi,
    wq_sem, wo_sem,
    az_s, az_r, sz_s, sz_r, mz_s, mz_r, bx_s, bx_r, bc_s, bc_r, sx_s, sx_r, cc_s, cc_r,
    ch_s, ch_r, at_s, at_r, pc_s, pc_r, px_s, px_r, pz_s, pz_r,
):
    nt, ns, nm, tok, db, heads_cols, pc, nw = cfg
    tokh = tok // nm
    seq_len = tok * ns
    half = nt // 2
    groups = heads_cols // pc
    pieces = 3 * groups
    chunks = db // nw
    t, s, m = lax.axis_index("tm"), lax.axis_index("seq"), lax.axis_index("mp")
    om = 1 - m
    width = db * nt

    for j in range(groups):
        for c in range(3):
            pltpu.make_async_copy(
                w_qkv.at[c, :, pl.ds(j * pc, pc)], wq.at[j * 3 + c], wq_sem.at[j * 3 + c]
            ).start()
    for n in range(chunks):
        for j in range(groups):
            pltpu.make_async_copy(
                w_out.at[pl.ds(n * nw, nw), pl.ds(j * pc, pc)], wo.at[n, j], wo_sem.at[n, j]
            ).start()

    barrier = pltpu.get_barrier_semaphore()

    def greet(**where):
        pl.semaphore_signal(barrier, inc=1, device_id=where, device_id_type=MESH)

    for k in range(1, nt):
        greet(tm=lax.rem(t + k, nt), mp=m)
    for k in range(nt):
        greet(tm=lax.rem(t + k, nt), mp=om)
    for k in range(1, ns):
        greet(seq=lax.rem(s + k, ns))
    pl.semaphore_wait(barrier, 2 * nt - 1 + ns - 1)

    zs = [lax.rem(t + k, nt) for k in range(nt)]
    xs = [lax.rem(s + k, ns) for k in range(ns)]

    def az(k):
        return remote(xb.at[zs[k], m], xin.at[t, s, m], az_s.at[k], az_r.at[t], tm=zs[k])

    def sz(k):
        return remote(st_out, st_in.at[t, s], sz_s.at[k], sz_r.at[t], tm=zs[k])

    def mz(k):
        return remote(modp.at[zs[k]], mod_in.at[t], mz_s.at[k], mz_r.at[t], tm=zs[k])

    for k in range(1, nt):
        az(k).start()
    for k in range(1, nt):
        mz(k).start()
    xin[t, s] = xb[t]
    mod_in[t] = modp[t]

    def bx(tt, k):
        ref = xin.at[tt, s, m]
        return remote(ref, ref, bx_s.at[tt, k], bx_r.at[tt, s], seq=xs[k])

    def bc(tt):
        ref = xin.at[tt, s, m]
        return remote(ref, ref, bc_s.at[tt], bc_r.at[tt], mp=om)

    def sx(tt, k):
        ref = st_in.at[tt, s]
        return remote(ref, ref, sx_s.at[tt, k], sx_r.at[tt, s], seq=xs[k])

    def cc(tt, k):
        ref = xin.at[tt, xs[k], m]
        return remote(ref, ref, cc_s.at[tt, k], cc_r.at[tt, xs[k]], mp=om)

    for k in range(1, ns):
        bx(t, k).start()

    total = jnp.zeros((tok, 1), F32)
    for b in range(nt):
        total += jnp.sum(xb[b].reshape(tok, db).astype(F32), axis=-1, keepdims=True)
    mean = total / width
    total = jnp.zeros((tok, 1), F32)
    for b in range(nt):
        centred = xb[b].reshape(tok, db).astype(F32) - mean
        total += jnp.sum(centred * centred, axis=-1, keepdims=True)
    rstd = lax.rsqrt(total / width + norm_eps)
    lane = lax.broadcasted_iota(jnp.int32, (tok, 128), 1)
    both = jnp.where(lane == 0, mean, jnp.where(lane == 1, rstd, 0.0))
    if tok < 128:
        both = jnp.concatenate([both, jnp.zeros((128 - tok, 128), F32)], axis=0)
    st_out[...] = both.T[:8, :]
    st_in[t, s] = st_out[...]
    for k in range(1, nt):
        sz(k).start()
    for k in range(1, ns):
        sx(t, k).start()

    for k in range(1, nt):
        tt = zs[k]
        ref = xin.at[tt, s, m]
        remote(ref, ref, az_s.at[k], az_r.at[tt], tm=tt).wait_recv()
        for i in range(1, ns):
            bx(tt, i).start()
        bc(tt).start()
    for k in range(1, nt):
        tt = zs[k]
        ref = st_in.at[tt, s]
        remote(ref, ref, sz_s.at[k], sz_r.at[tt], tm=tt).wait_recv()
        for i in range(1, ns):
            sx(tt, i).start()
    for k in range(nt):
        tt = zs[k]
        for i in range(1, ns):
            ref = xin.at[tt, xs[i], m]
            remote(ref, ref, bx_s.at[tt, i], bx_r.at[tt, xs[i]], seq=xs[i]).wait_recv()
            cc(tt, i).start()

    for k in range(1, nt):
        tt = zs[k]
        ref = mod_in.at[tt]
        remote(ref, ref, mz_s.at[k], mz_r.at[tt], tm=tt).wait_recv()
    total = mod_in[0]
    for b in range(1, nt):
        total = total + mod_in[b]
    mods[...] = total

    for k in range(nt):
        tt = zs[k]
        if k > 0:
            ref = xin.at[tt, s, om]
            remote(ref, ref, bc_s.at[tt], bc_r.at[tt], mp=om).wait_recv()
        for i in range(1, ns):
            ref = xin.at[tt, xs[i], om]
            remote(ref, ref, cc_s.at[tt, i], cc_r.at[tt, xs[i]], mp=om).wait_recv()
            ref = st_in.at[tt, xs[i]]
            remote(ref, ref, sx_s.at[tt, i], sx_r.at[tt, xs[i]], seq=xs[i]).wait_recv()

    def modulate(tt, carry):
        shift = mods[0, pl.ds(tt, 1), :]
        scale = mods[1, pl.ds(tt, 1), :]
        for ss in range(ns):
            stats = st_in[tt, ss].T
            x = xin[tt, ss].reshape(tok, db).astype(F32)
            normed = (x - stats[:tok, 0:1]) * stats[:tok, 1:2]
            hid[tt, pl.ds(ss * tok, tok), :] = (normed * (1.0 + scale) + shift).astype(BF16)
        return carry

    lax.fori_loop(0, nt, modulate, 0)

    def ch(p, d, h):
        ref = chain.at[p, d, h]
        dest = jnp.minimum(t + 1, nt - 1) if d == 1 else jnp.maximum(t - 1, 0)
        return remote(ref, ref, ch_s.at[p, d, h], ch_r.at[p, d, h], tm=dest)

    per = max(1, min(half, 256 // seq_len))

    def project(p, carry):
        pltpu.make_async_copy(w_qkv.at[0, :, pl.ds(0, pc)], wq.at[p], wq_sem.at[p]).wait()
        for d in range(2):
            is_first = t == (0 if d == 1 else nt - 1)

            def rows(g, c2):
                lhs = hid[pl.ds(d * half + g * per, per)].reshape(per * seq_len, db)
                prod = jnp.dot(lhs, wq[p], preferred_element_type=F32)
                prod = prod.reshape(per, seq_len, pc)
                own[p, d, pl.ds(g * per, per)] = prod

                @pl.when(is_first)
                def _():
                    chain[p, d, pl.ds(g * per, per)] = prod.astype(BF16)
                    for h in range(per):
                        ch(p, d, g * per + h).start()

                return c2

            lax.fori_loop(0, half // per, rows, 0)

        return carry

    lax.fori_loop(0, pieces, project, 0)

    inv_root = 1.0 / jnp.sqrt(F32(HEAD_DIM))

    def at_copy(j, d, h):
        ref = at.at[d, j, h]
        dest = jnp.maximum(t - 1, 0) if d == 1 else jnp.minimum(t + 1, nt - 1)
        return remote(ref, ref, at_s.at[d, j, h], at_r.at[d, j, h], tm=dest)

    def find_probs(j, d, h):
        for i in range(pc // HEAD_DIM):
            cols = slice(i * HEAD_DIM, (i + 1) * HEAD_DIM)

            def normed(which):
                v = own[3 * j + which, d, h, :, cols]
                meansq = jnp.mean(v * v, axis=-1, keepdims=True)
                g = gains[which, j, :, cols]
                return (v * lax.rsqrt(meansq + norm_eps) * g).astype(BF16)

            scores = lax.dot_general(
                normed(0), normed(1), (((1,), (1,)), ((), ())), preferred_element_type=F32
            ) * inv_root
            expo = jnp.exp(scores)
            probs_ref[h, i] = (expo / jnp.sum(expo, axis=-1, keepdims=True)).astype(BF16)

    def attend(j, d, h):
        for i in range(pc // HEAD_DIM):
            cols = slice(i * HEAD_DIM, (i + 1) * HEAD_DIM)
            v = own[3 * j + 2, d, h, :, cols].astype(BF16)
            at[d, j, h, :, cols] = jnp.dot(
                probs_ref[h, i], v, preferred_element_type=F32
            ).astype(BF16)

    steps = pieces * half
    skew, slack = 4, 3

    def chain_step(k, carry):
        for d in range(2):
            lag = skew * (t - 1 if d == 1 else nt - 2 - t)
            i = k - lag
            last = t == (nt - 1 if d == 1 else 0)

            @pl.when((lag >= 0) & (i >= 0) & (i < steps))
            def _():
                p, h = i // half, lax.rem(i, half)
                ref = chain.at[p, d, h]
                remote(ref, ref, ch_s.at[p, d, h], ch_r.at[p, d, h], mp=om).wait_recv()

                @pl.when(jnp.logical_not(last))
                def _():
                    chain[p, d, h] = (chain[p, d, h].astype(F32) + own[p, d, h]).astype(BF16)
                    ch(p, d, h).start()

                @pl.when(last)
                def _():
                    own[p, d, h] = chain[p, d, h].astype(F32) + own[p, d, h]
                    which, j = lax.rem(p, 3), p // 3

                    @pl.when(which == 1)
                    def _():
                        find_probs(j, d, h)

                    @pl.when(which == 2)
                    def _():
                        attend(j, d, h)
                        at_copy(j, d, h).start()

        for d in range(2):
            behind = nt - 1 - t if d == 1 else t
            i = k - skew * (nt - 2) - slack * behind
            p, h = jnp.maximum(i, 0) // half, lax.rem(jnp.maximum(i, 0), half)

            @pl.when((behind > 0) & (i >= 0) & (i < steps) & (lax.rem(p, 3) == 2))
            def _():
                j = p // 3
                ref = at.at[d, j, h]
                remote(ref, ref, at_s.at[d, j, h], at_r.at[d, j, h], mp=om).wait_recv()

                @pl.when(behind < nt - 1)
                def _():
                    at_copy(j, d, h).start()

        return carry

    lax.fori_loop(0, steps + skew * (nt - 2) + slack * (nt - 1), chain_step, 0)

    def pcopy(n):
        return remote(pp.at[n, om], sib.at[n], pc_s.at[n], pc_r.at[n], mp=om)

    def px(n, k):
        return remote(xo.at[n, xs[k]], xi.at[n, s], px_s.at[n, k], px_r.at[n, s], seq=xs[k])

    blocks = nt // nm
    om_t = t // blocks
    blk = lax.rem(t, blocks)

    def pz(n, tt):
        return remote(
            zo.at[n, tt], zi.at[n, blk, m], pz_s.at[n, tt], pz_r.at[n, blk, m], tm=tt, mp=om_t
        )

    for n in range(chunks):
        for j in range(groups):
            pltpu.make_async_copy(
                w_out.at[pl.ds(n * nw, nw), pl.ds(j * pc, pc)], wo.at[n, j], wo_sem.at[n, j]
            ).wait()
        run[...] = jnp.zeros_like(run)
        for d in range(2):
            def one_step(h, carry):
                tt = d * half + h
                acc = jnp.zeros((seq_len, nw), F32)
                for j in range(groups):
                    acc += lax.dot_general(
                        at[d, j, h], wo[n, j], (((1,), (1,)), ((), ())), preferred_element_type=F32
                    )
                gate = mods[2, pl.ds(tt, 1), n * nw:(n + 1) * nw]
                gate = gate * dtb[pl.ds(tt, 1), n * nw:(n + 1) * nw]
                new = run[...] + gate * acc
                run[...] = new
                parted = new.reshape(ns, nm, tokh, nw)
                for hh in range(nm):
                    pp[n, hh, tt] = parted[:, hh]
                return carry

            lax.fori_loop(0, half, one_step, 0)
        pcopy(n).start()

    for n in range(chunks):
        pcopy(n).wait_recv()

        def add(tt, carry):
            both = pp[n, m, tt] + sib[n, tt]
            pp[n, m, tt] = both
            for ss in range(ns):
                xo[n, ss, tt] = both[ss].astype(BF16)
            return carry

        lax.fori_loop(0, nt, add, 0)
        for k in range(1, ns):
            px(n, k).start()

    def to_owner(n, tt, act):
        @pl.when(jnp.logical_not((tt == t) & (om_t == m)))
        def _():
            act(pz(n, tt))

    for n in range(chunks):
        for k in range(1, ns):
            ref = xi.at[n, xs[k]]
            remote(ref, ref, px_s.at[n, k], px_r.at[n, xs[k]], seq=xs[k]).wait_recv()

        def finish(tt, carry):
            whole = pp[n, m, tt, s]
            for k in range(1, ns):
                whole = whole + xi[n, xs[k], tt].astype(F32)
            zo[n, tt] = whole
            to_owner(n, tt, lambda c: c.start())
            return carry

        lax.fori_loop(0, nt, finish, 0)

    @pl.when(om_t == m)
    def _():
        for n in range(chunks):
            zi[n, blk, m] = zo[n, t]

    for n in range(chunks):
        for b in range(blocks):
            for mm in range(nm):
                here = (m * blocks + b == t) & (m == mm)
                ref = zi.at[n, b, mm]

                @pl.when(jnp.logical_not(here))
                def _():
                    remote(ref, ref, pz_s.at[n, 0], pz_r.at[n, b, mm], mp=om).wait_recv()

                out[b, mm * tokh:(mm + 1) * tokh, n * nw:(n + 1) * nw] = zi[n, b, mm]

    for k in range(1, nt):
        az(k).wait_send()
        mz(k).wait_send()
        sz(k).wait_send()
        bc(zs[k]).wait_send()
    for k in range(nt):
        for i in range(1, ns):
            bx(zs[k], i).wait_send()
            sx(zs[k], i).wait_send()
            cc(zs[k], i).wait_send()
    for d in range(2):
        last = t == (nt - 1 if d == 1 else 0)
        far = t == (0 if d == 1 else nt - 1)

        @pl.when(jnp.logical_not(last))
        def _():
            def body(p, carry):
                for h in range(half):
                    ch(p, d, h).wait_send()
                return carry

            lax.fori_loop(0, pieces, body, 0)

        @pl.when(jnp.logical_not(far))
        def _():
            def body(j, carry):
                for h in range(half):
                    at_copy(j, d, h).wait_send()
                return carry

            lax.fori_loop(0, groups, body, 0)
    for n in range(chunks):
        pcopy(n).wait_send()
        for k in range(1, ns):
            px(n, k).wait_send()

        def body(tt, carry):
            to_owner(n, tt, lambda c: c.wait_send())
            return carry

        lax.fori_loop(0, nt, body, 0)


def on_device(states, start_step, w_qkv, qk_gain, w_out, time_proj):
    _, tok, width = states.shape
    nt = lax.axis_size("tm")
    ns = lax.axis_size("seq")
    nm = lax.axis_size("mp")
    tm_pos = lax.axis_index("tm")
    db = width // nt
    heads_cols = w_qkv.shape[2]
    pc = 256 if heads_cols % 256 == 0 else heads_cols
    nw = 256 if db % 256 == 0 else db
    tokh = tok // nm
    seq_len = tok * ns
    half = nt // 2
    groups = heads_cols // pc
    pieces = 3 * groups
    chunks = db // nw
    blocks = nt // nm

    steps_idx = start_step[0] + jnp.arange(nt)
    sigma_now = sigma_of(steps_idx)
    step_size = sigma_of(steps_idx + 1) - sigma_now
    emb = embed_time(sigma_now)
    freq_rows = time_proj.shape[0]
    emb_cols = lax.dynamic_slice_in_dim(emb, tm_pos * freq_rows, freq_rows, 1)
    modp = jnp.dot(emb_cols, time_proj, preferred_element_type=F32)
    modp = modp.reshape(nt, 3, nt, db).transpose(2, 1, 0, 3)
    dtb = jnp.broadcast_to(step_size[:, None], (nt, db))
    xb = states.reshape(nm, tokh, nt, db).transpose(2, 0, 1, 3)
    gains = qk_gain.reshape(2, groups, 1, pc)

    dma = pltpu.SemaphoreType.DMA
    vmem = pltpu.VMEM
    cfg = (nt, ns, nm, tok, db, heads_cols, pc, nw)
    result = pl.pallas_call(
        functools.partial(sweep_kernel, cfg),
        out_shape=jax.ShapeDtypeStruct((blocks, tok, db), F32),
        in_specs=[pl.BlockSpec(memory_space=pltpu.VMEM)] * 4
        + [pl.BlockSpec(memory_space=pl.ANY)] * 2,
        out_specs=pl.BlockSpec(memory_space=pltpu.VMEM),
        scratch_shapes=[
            vmem((nt, ns, nm, tokh, db), BF16),
            vmem((8, 128), F32),
            vmem((nt, ns, 8, 128), F32),
            vmem((nt, 3, nt, db), F32),
            vmem((3, nt, db), F32),
            vmem((nt, seq_len, db), BF16),
            vmem((pieces, db, pc), BF16),
            vmem((chunks, groups, nw, pc), BF16),
            vmem((pieces, 2, half, seq_len, pc), F32),
            vmem((pieces, 2, half, seq_len, pc), BF16),
            vmem((half, pc // HEAD_DIM, seq_len, seq_len), BF16),
            vmem((2, groups, half, seq_len, pc), BF16),
            vmem((seq_len, nw), F32),
            vmem((chunks, nm, nt, ns, tokh, nw), F32),
            vmem((chunks, nt, ns, tokh, nw), F32),
            vmem((chunks, ns, nt, tokh, nw), BF16),
            vmem((chunks, ns, nt, tokh, nw), BF16),
            vmem((chunks, nt, tokh, nw), F32),
            vmem((chunks, blocks, nm, tokh, nw), F32),
            dma((pieces,)),
            dma((chunks, groups)),
            dma((nt,)), dma((nt,)),
            dma((nt,)), dma((nt,)),
            dma((nt,)), dma((nt,)),
            dma((nt, ns)), dma((nt, ns)),
            dma((nt,)), dma((nt,)),
            dma((nt, ns)), dma((nt, ns)),
            dma((nt, ns)), dma((nt, ns)),
            dma((pieces, 2, half)), dma((pieces, 2, half)),
            dma((2, groups, half)), dma((2, groups, half)),
            dma((chunks,)), dma((chunks,)),
            dma((chunks, ns)), dma((chunks, ns)),
            dma((chunks, nt)), dma((chunks, blocks, nm)),
        ],
        compiler_params=pltpu.CompilerParams(
            collective_id=0, has_side_effects=True, vmem_limit_bytes=60 * 1024 * 1024
        ),
    )(xb, modp, dtb, gains, w_qkv, w_out)
    return result.transpose(1, 0, 2).reshape(1, tok, blocks * db)


def solution(mesh):
    return jax.shard_map(
        on_device,
        mesh=mesh,
        in_specs=(
            P(("group", "tm"), "seq", None),
            P("group"),
            P(None, "tm", ("seq", "mp")),
            P(None, ("seq", "mp")),
            P("tm", ("seq", "mp")),
            P("tm", None),
        ),
        out_specs=P(("group", "tm"), "seq", "mp"),
        check_vma=False,
    )
```

```python
import functools

import jax
import jax.numpy as jnp
from jax import lax
from jax.experimental import pallas as pl
from jax.experimental.pallas import tpu as pltpu
from jax.sharding import PartitionSpec as P

HEAD_DIM = 128
FREQ = 256
STEPS = 100

sample_shift = 5.0
norm_eps = 1e-06

MESH = pl.DeviceIdType.MESH
F32 = jnp.float32
BF16 = jnp.bfloat16


def sigma_of(index):
    unit = 1.0 - index.astype(jnp.float32) / jnp.float32(STEPS)
    return sample_shift * unit / (1.0 + (sample_shift - 1.0) * unit)


def embed_time(sigma_now):
    half_freq = FREQ // 2
    ranks = jnp.arange(half_freq).astype(jnp.float32)
    freqs = jnp.exp(-jnp.log(jnp.float32(10000.0)) * ranks / jnp.float32(half_freq))
    angles = (1000.0 * sigma_now)[:, None] * freqs[None, :]
    return jnp.concatenate([jnp.cos(angles), jnp.sin(angles)], axis=1).astype(jnp.bfloat16)


def remote(src, dst, send_sem, recv_sem, **where):
    return pltpu.make_async_remote_copy(
        src_ref=src, dst_ref=dst, send_sem=send_sem, recv_sem=recv_sem,
        device_id=where, device_id_type=MESH,
    )


def sweep_kernel(
    cfg, xb, modp, dtb, gains, w_qkv, w_out, out,
    xin, st_out, st_in, mod_in, mods, hid, wq, wo, own, chain, probs_ref, at, run, pp, sib, xo, xi, zo, zi,
    wq_sem, wo_sem,
    az_s, az_r, sz_s, sz_r, mz_s, mz_r, bx_s, bx_r, bc_s, bc_r, sx_s, sx_r, cc_s, cc_r,
    ch_s, ch_r, at_s, at_r, pc_s, pc_r, px_s, px_r, pz_s, pz_r,
):
    nt, ns, nm, tok, db, heads_cols, pc, nw = cfg
    tokh = tok // nm
    seq_len = tok * ns
    half = nt // 2
    groups = heads_cols // pc
    pieces = 3 * groups
    chunks = db // nw
    t, s, m = lax.axis_index("tm"), lax.axis_index("seq"), lax.axis_index("mp")
    om = 1 - m
    width = db * nt

    for j in range(groups):
        for c in range(3):
            pltpu.make_async_copy(
                w_qkv.at[c, :, pl.ds(j * pc, pc)], wq.at[j * 3 + c], wq_sem.at[j * 3 + c]
            ).start()
    for n in range(chunks):
        for j in range(groups):
            pltpu.make_async_copy(
                w_out.at[pl.ds(n * nw, nw), pl.ds(j * pc, pc)], wo.at[n, j], wo_sem.at[n, j]
            ).start()

    barrier = pltpu.get_barrier_semaphore()

    def greet(**where):
        pl.semaphore_signal(barrier, inc=1, device_id=where, device_id_type=MESH)

    for k in range(1, nt):
        greet(tm=lax.rem(t + k, nt), mp=m)
    for k in range(nt):
        greet(tm=lax.rem(t + k, nt), mp=om)
    for k in range(1, ns):
        greet(seq=lax.rem(s + k, ns))
    pl.semaphore_wait(barrier, 2 * nt - 1 + ns - 1)

    zs = [lax.rem(t + k, nt) for k in range(nt)]
    xs = [lax.rem(s + k, ns) for k in range(ns)]

    def az(k):
        return remote(xb.at[zs[k], m], xin.at[t, s, m], az_s.at[k], az_r.at[t], tm=zs[k])

    def sz(k):
        return remote(st_out, st_in.at[t, s], sz_s.at[k], sz_r.at[t], tm=zs[k])

    def mz(k):
        return remote(modp.at[zs[k]], mod_in.at[t], mz_s.at[k], mz_r.at[t], tm=zs[k])

    for k in range(1, nt):
        az(k).start()
    for k in range(1, nt):
        mz(k).start()
    xin[t, s] = xb[t]
    mod_in[t] = modp[t]

    def bx(tt, k):
        ref = xin.at[tt, s, m]
        return remote(ref, ref, bx_s.at[tt, k], bx_r.at[tt, s], seq=xs[k])

    def bc(tt):
        ref = xin.at[tt, s, m]
        return remote(ref, ref, bc_s.at[tt], bc_r.at[tt], mp=om)

    def sx(tt, k):
        ref = st_in.at[tt, s]
        return remote(ref, ref, sx_s.at[tt, k], sx_r.at[tt, s], seq=xs[k])

    def cc(tt, k):
        ref = xin.at[tt, xs[k], m]
        return remote(ref, ref, cc_s.at[tt, k], cc_r.at[tt, xs[k]], mp=om)

    for k in range(1, ns):
        bx(t, k).start()

    total = jnp.zeros((tok, 1), F32)
    for b in range(nt):
        total += jnp.sum(xb[b].reshape(tok, db).astype(F32), axis=-1, keepdims=True)
    mean = total / width
    total = jnp.zeros((tok, 1), F32)
    for b in range(nt):
        centred = xb[b].reshape(tok, db).astype(F32) - mean
        total += jnp.sum(centred * centred, axis=-1, keepdims=True)
    rstd = lax.rsqrt(total / width + norm_eps)
    lane = lax.broadcasted_iota(jnp.int32, (tok, 128), 1)
    both = jnp.where(lane == 0, mean, jnp.where(lane == 1, rstd, 0.0))
    if tok < 128:
        both = jnp.concatenate([both, jnp.zeros((128 - tok, 128), F32)], axis=0)
    st_out[...] = both.T[:8, :]
    st_in[t, s] = st_out[...]
    for k in range(1, nt):
        sz(k).start()
    for k in range(1, ns):
        sx(t, k).start()

    for k in range(1, nt):
        tt = zs[k]
        ref = xin.at[tt, s, m]
        remote(ref, ref, az_s.at[k], az_r.at[tt], tm=tt).wait_recv()
        for i in range(1, ns):
            bx(tt, i).start()
        bc(tt).start()
    for k in range(1, nt):
        tt = zs[k]
        ref = st_in.at[tt, s]
        remote(ref, ref, sz_s.at[k], sz_r.at[tt], tm=tt).wait_recv()
        for i in range(1, ns):
            sx(tt, i).start()
    for k in range(nt):
        tt = zs[k]
        for i in range(1, ns):
            ref = xin.at[tt, xs[i], m]
            remote(ref, ref, bx_s.at[tt, i], bx_r.at[tt, xs[i]], seq=xs[i]).wait_recv()
            cc(tt, i).start()

    for k in range(1, nt):
        tt = zs[k]
        ref = mod_in.at[tt]
        remote(ref, ref, mz_s.at[k], mz_r.at[tt], tm=tt).wait_recv()
    total = mod_in[0]
    for b in range(1, nt):
        total = total + mod_in[b]
    mods[...] = total

    for k in range(nt):
        tt = zs[k]
        if k > 0:
            ref = xin.at[tt, s, om]
            remote(ref, ref, bc_s.at[tt], bc_r.at[tt], mp=om).wait_recv()
        for i in range(1, ns):
            ref = xin.at[tt, xs[i], om]
            remote(ref, ref, cc_s.at[tt, i], cc_r.at[tt, xs[i]], mp=om).wait_recv()
            ref = st_in.at[tt, xs[i]]
            remote(ref, ref, sx_s.at[tt, i], sx_r.at[tt, xs[i]], seq=xs[i]).wait_recv()

    def modulate(tt, carry):
        shift = mods[0, pl.ds(tt, 1), :]
        scale = mods[1, pl.ds(tt, 1), :]
        for ss in range(ns):
            stats = st_in[tt, ss].T
            x = xin[tt, ss].reshape(tok, db).astype(F32)
            normed = (x - stats[:tok, 0:1]) * stats[:tok, 1:2]
            hid[tt, pl.ds(ss * tok, tok), :] = (normed * (1.0 + scale) + shift).astype(BF16)
        return carry

    lax.fori_loop(0, nt, modulate, 0)

    def ch(p, d, h):
        ref = chain.at[p, d, h]
        dest = jnp.minimum(t + 1, nt - 1) if d == 1 else jnp.maximum(t - 1, 0)
        return remote(ref, ref, ch_s.at[p, d, h], ch_r.at[p, d, h], tm=dest)

    per = max(1, min(half, 256 // seq_len))

    def project(p, carry):
        pltpu.make_async_copy(w_qkv.at[0, :, pl.ds(0, pc)], wq.at[p], wq_sem.at[p]).wait()
        for d in range(2):
            is_first = t == (0 if d == 1 else nt - 1)

            def rows(g, c2):
                lhs = hid[pl.ds(d * half + g * per, per)].reshape(per * seq_len, db)
                prod = jnp.dot(lhs, wq[p], preferred_element_type=F32)
                prod = prod.reshape(per, seq_len, pc)
                own[p, d, pl.ds(g * per, per)] = prod

                @pl.when(is_first)
                def _():
                    chain[p, d, pl.ds(g * per, per)] = prod.astype(BF16)
                    for h in range(per):
                        ch(p, d, g * per + h).start()

                return c2

            lax.fori_loop(0, half // per, rows, 0)

        return carry


    inv_root = 1.0 / jnp.sqrt(F32(HEAD_DIM))

    def at_copy(j, d, h):
        ref = at.at[d, j, h]
        dest = jnp.maximum(t - 1, 0) if d == 1 else jnp.minimum(t + 1, nt - 1)
        return remote(ref, ref, at_s.at[d, j, h], at_r.at[d, j, h], tm=dest)

    def find_probs(j, d, h):
        for i in range(pc // HEAD_DIM):
            cols = slice(i * HEAD_DIM, (i + 1) * HEAD_DIM)

            def normed(which):
                v = own[3 * j + which, d, h, :, cols]
                meansq = jnp.mean(v * v, axis=-1, keepdims=True)
                first = pl.multiple_of(j * pc + i * HEAD_DIM, HEAD_DIM)
                g = gains[which:which + 1, pl.ds(first, HEAD_DIM)]
                return (v * lax.rsqrt(meansq + norm_eps) * g).astype(BF16)

            scores = lax.dot_general(
                normed(0), normed(1), (((1,), (1,)), ((), ())), preferred_element_type=F32
            ) * inv_root
            expo = jnp.exp(scores)
            probs_ref[h, i] = (expo / jnp.sum(expo, axis=-1, keepdims=True)).astype(BF16)

    def attend(j, d, h):
        for i in range(pc // HEAD_DIM):
            cols = slice(i * HEAD_DIM, (i + 1) * HEAD_DIM)
            v = own[3 * j + 2, d, h, :, cols].astype(BF16)
            at[d, j, h, :, cols] = jnp.dot(
                probs_ref[h, i], v, preferred_element_type=F32
            ).astype(BF16)

    steps = pieces * half
    skew, slack = 4, 3

    def chain_step(k, carry):
        @pl.when(k < pieces)
        def _():
            project(k, 0)

        for d in range(2):
            lag = skew * (t - 1 if d == 1 else nt - 2 - t)
            i = k - lag
            last = t == (nt - 1 if d == 1 else 0)

            @pl.when((lag >= 0) & (i >= 0) & (i < steps))
            def _():
                p, h = i // half, lax.rem(i, half)
                ref = chain.at[p, d, h]
                remote(ref, ref, ch_s.at[p, d, h], ch_r.at[p, d, h], mp=om).wait_recv()

                @pl.when(jnp.logical_not(last))
                def _():
                    chain[p, d, h] = (chain[p, d, h].astype(F32) + own[p, d, h]).astype(BF16)
                    ch(p, d, h).start()

                @pl.when(last)
                def _():
                    own[p, d, h] = chain[p, d, h].astype(F32) + own[p, d, h]
                    which, j = lax.rem(p, 3), p // 3

                    @pl.when(which == 1)
                    def _():
                        find_probs(j, d, h)

                    @pl.when(which == 2)
                    def _():
                        attend(j, d, h)
                        at_copy(j, d, h).start()

        for d in range(2):
            behind = nt - 1 - t if d == 1 else t
            i = k - skew * (nt - 2) - slack * behind
            p, h = jnp.maximum(i, 0) // half, lax.rem(jnp.maximum(i, 0), half)

            @pl.when((behind > 0) & (i >= 0) & (i < steps) & (lax.rem(p, 3) == 2))
            def _():
                j = p // 3
                ref = at.at[d, j, h]
                remote(ref, ref, at_s.at[d, j, h], at_r.at[d, j, h], mp=om).wait_recv()

                @pl.when(behind < nt - 1)
                def _():
                    at_copy(j, d, h).start()

        return carry

    lax.fori_loop(0, steps + skew * (nt - 2) + slack * (nt - 1), chain_step, 0)

    def pcopy(n):
        return remote(pp.at[n, om], sib.at[n], pc_s.at[n], pc_r.at[n], mp=om)

    def px(n, k):
        return remote(xo.at[n, xs[k]], xi.at[n, s], px_s.at[n, k], px_r.at[n, s], seq=xs[k])

    blocks = nt // nm
    om_t = t // blocks
    blk = lax.rem(t, blocks)

    def pz(n, tt):
        return remote(
            zo.at[n, tt], zi.at[n, blk, m], pz_s.at[n, tt], pz_r.at[n, blk, m], tm=tt, mp=om_t
        )

    def produce(n):
        for j in range(groups):
            pltpu.make_async_copy(
                w_out.at[pl.ds(n * nw, nw), pl.ds(j * pc, pc)], wo.at[n, j], wo_sem.at[n, j]
            ).wait()
        run[...] = jnp.zeros_like(run)
        for d in range(2):
            def one_step(h, carry):
                tt = d * half + h
                acc = jnp.zeros((seq_len, nw), F32)
                for j in range(groups):
                    acc += lax.dot_general(
                        at[d, j, h], wo[n, j], (((1,), (1,)), ((), ())), preferred_element_type=F32
                    )
                gate = mods[2, pl.ds(tt, 1), n * nw:(n + 1) * nw]
                gate = gate * dtb[pl.ds(tt, 1), n * nw:(n + 1) * nw]
                new = run[...] + gate * acc
                run[...] = new
                parted = new.reshape(ns, nm, tokh, nw)
                for hh in range(nm):
                    pp[n, hh, tt] = parted[:, hh]
                return carry

            lax.fori_loop(0, half, one_step, 0)
        pcopy(n).start()

    def fold(n):
        pcopy(n).wait_recv()

        def add(tt, carry):
            both = pp[n, m, tt] + sib[n, tt]
            pp[n, m, tt] = both
            for ss in range(ns):
                xo[n, ss, tt] = both[ss].astype(BF16)
            return carry

        lax.fori_loop(0, nt, add, 0)
        for k in range(1, ns):
            px(n, k).start()

    def to_owner(n, tt, act):
        @pl.when(jnp.logical_not((tt == t) & (om_t == m)))
        def _():
            act(pz(n, tt))

    def deliver(n):
        for k in range(1, ns):
            ref = xi.at[n, xs[k]]
            remote(ref, ref, px_s.at[n, k], px_r.at[n, xs[k]], seq=xs[k]).wait_recv()

        def finish(tt, carry):
            whole = pp[n, m, tt, s]
            for k in range(1, ns):
                whole = whole + xi[n, xs[k], tt].astype(F32)
            zo[n, tt] = whole
            to_owner(n, tt, lambda c: c.start())
            return carry

        lax.fori_loop(0, nt, finish, 0)

    for n in range(chunks + 2):
        if n < chunks:
            produce(n)
        if 0 <= n - 1 < chunks:
            fold(n - 1)
        if 0 <= n - 2 < chunks:
            deliver(n - 2)

    @pl.when(om_t == m)
    def _():
        for n in range(chunks):
            zi[n, blk, m] = zo[n, t]

    for n in range(chunks):
        for b in range(blocks):
            for mm in range(nm):
                here = (m * blocks + b == t) & (m == mm)
                ref = zi.at[n, b, mm]

                @pl.when(jnp.logical_not(here))
                def _():
                    remote(ref, ref, pz_s.at[n, 0], pz_r.at[n, b, mm], mp=om).wait_recv()

                out[mm * tokh:(mm + 1) * tokh, b * db + n * nw:b * db + (n + 1) * nw] = zi[n, b, mm]

    for k in range(1, nt):
        az(k).wait_send()
        mz(k).wait_send()
        sz(k).wait_send()
        bc(zs[k]).wait_send()
    for k in range(nt):
        for i in range(1, ns):
            bx(zs[k], i).wait_send()
            sx(zs[k], i).wait_send()
            cc(zs[k], i).wait_send()
    for d in range(2):
        last = t == (nt - 1 if d == 1 else 0)
        far = t == (0 if d == 1 else nt - 1)

        @pl.when(jnp.logical_not(last))
        def _():
            def body(p, carry):
                for h in range(half):
                    ch(p, d, h).wait_send()
                return carry

            lax.fori_loop(0, pieces, body, 0)

        @pl.when(jnp.logical_not(far))
        def _():
            def body(j, carry):
                for h in range(half):
                    at_copy(j, d, h).wait_send()
                return carry

            lax.fori_loop(0, groups, body, 0)
    for n in range(chunks):
        pcopy(n).wait_send()
        for k in range(1, ns):
            px(n, k).wait_send()

        def body(tt, carry):
            to_owner(n, tt, lambda c: c.wait_send())
            return carry

        lax.fori_loop(0, nt, body, 0)


def on_device(states, start_step, w_qkv, qk_gain, w_out, time_proj):
    _, tok, width = states.shape
    nt = lax.axis_size("tm")
    ns = lax.axis_size("seq")
    nm = lax.axis_size("mp")
    tm_pos = lax.axis_index("tm")
    db = width // nt
    heads_cols = w_qkv.shape[2]
    pc = 256 if heads_cols % 256 == 0 else heads_cols
    nw = 256 if db % 256 == 0 else db
    tokh = tok // nm
    seq_len = tok * ns
    half = nt // 2
    groups = heads_cols // pc
    pieces = 3 * groups
    chunks = db // nw
    blocks = nt // nm

    steps_idx = start_step[0] + jnp.arange(nt)
    sigma_now = sigma_of(steps_idx)
    step_size = sigma_of(steps_idx + 1) - sigma_now
    emb = embed_time(sigma_now)
    freq_rows = time_proj.shape[0]
    emb_cols = lax.dynamic_slice_in_dim(emb, tm_pos * freq_rows, freq_rows, 1)
    modp = jnp.dot(emb_cols, time_proj, preferred_element_type=F32)
    modp = modp.reshape(nt, 3, nt, db).transpose(2, 1, 0, 3)
    dtb = jnp.broadcast_to(step_size[:, None], (nt, db))
    xb = states.reshape(nm, tokh, nt, db).transpose(2, 0, 1, 3)

    dma = pltpu.SemaphoreType.DMA
    vmem = pltpu.VMEM
    cfg = (nt, ns, nm, tok, db, heads_cols, pc, nw)
    result = pl.pallas_call(
        functools.partial(sweep_kernel, cfg),
        out_shape=jax.ShapeDtypeStruct((tok, blocks * db), F32),
        in_specs=[pl.BlockSpec(memory_space=pltpu.VMEM)] * 4
        + [pl.BlockSpec(memory_space=pl.ANY)] * 2,
        out_specs=pl.BlockSpec(memory_space=pltpu.VMEM),
        scratch_shapes=[
            vmem((nt, ns, nm, tokh, db), BF16),
            vmem((8, 128), F32),
            vmem((nt, ns, 8, 128), F32),
            vmem((nt, 3, nt, db), F32),
            vmem((3, nt, db), F32),
            vmem((nt, seq_len, db), BF16),
            vmem((pieces, db, pc), BF16),
            vmem((chunks, groups, nw, pc), BF16),
            vmem((pieces, 2, half, seq_len, pc), F32),
            vmem((pieces, 2, half, seq_len, pc), BF16),
            vmem((half, pc // HEAD_DIM, seq_len, seq_len), BF16),
            vmem((2, groups, half, seq_len, pc), BF16),
            vmem((seq_len, nw), F32),
            vmem((chunks, nm, nt, ns, tokh, nw), F32),
            vmem((chunks, nt, ns, tokh, nw), F32),
            vmem((chunks, ns, nt, tokh, nw), BF16),
            vmem((chunks, ns, nt, tokh, nw), BF16),
            vmem((chunks, nt, tokh, nw), F32),
            vmem((chunks, blocks, nm, tokh, nw), F32),
            dma((pieces,)),
            dma((chunks, groups)),
            dma((nt,)), dma((nt,)),
            dma((nt,)), dma((nt,)),
            dma((nt,)), dma((nt,)),
            dma((nt, ns)), dma((nt, ns)),
            dma((nt,)), dma((nt,)),
            dma((nt, ns)), dma((nt, ns)),
            dma((nt, ns)), dma((nt, ns)),
            dma((pieces, 2, half)), dma((pieces, 2, half)),
            dma((2, groups, half)), dma((2, groups, half)),
            dma((chunks,)), dma((chunks,)),
            dma((chunks, ns)), dma((chunks, ns)),
            dma((chunks, nt)), dma((chunks, blocks, nm)),
        ],
        compiler_params=pltpu.CompilerParams(
            collective_id=0, has_side_effects=True, vmem_limit_bytes=60 * 1024 * 1024
        ),
    )(xb, modp, dtb, qk_gain, w_qkv, w_out)
    return result.reshape(1, tok, blocks * db)


def solution(mesh):
    return jax.shard_map(
        on_device,
        mesh=mesh,
        in_specs=(
            P(("group", "tm"), "seq", None),
            P("group"),
            P(None, "tm", ("seq", "mp")),
            P(None, ("seq", "mp")),
            P("tm", ("seq", "mp")),
            P("tm", None),
        ),
        out_specs=P(("group", "tm"), "seq", "mp"),
        check_vma=False,
    )
```

```python
import functools

import jax
import jax.numpy as jnp
from jax import lax
from jax.experimental import pallas as pl
from jax.experimental.pallas import tpu as pltpu
from jax.sharding import PartitionSpec as P

HEAD_DIM = 128
FREQ = 256
STEPS = 100

sample_shift = 5.0
norm_eps = 1e-06

MESH = pl.DeviceIdType.MESH
F32 = jnp.float32
BF16 = jnp.bfloat16


def sigma_of(index):
    unit = 1.0 - index.astype(jnp.float32) / jnp.float32(STEPS)
    return sample_shift * unit / (1.0 + (sample_shift - 1.0) * unit)


def embed_time(sigma_now):
    half_freq = FREQ // 2
    ranks = jnp.arange(half_freq).astype(jnp.float32)
    freqs = jnp.exp(-jnp.log(jnp.float32(10000.0)) * ranks / jnp.float32(half_freq))
    angles = (1000.0 * sigma_now)[:, None] * freqs[None, :]
    return jnp.concatenate([jnp.cos(angles), jnp.sin(angles)], axis=1).astype(jnp.bfloat16)


def remote(src, dst, send_sem, recv_sem, **where):
    return pltpu.make_async_remote_copy(
        src_ref=src, dst_ref=dst, send_sem=send_sem, recv_sem=recv_sem,
        device_id=where, device_id_type=MESH,
    )


def sweep_kernel(
    cfg, xb, modp, dtb, gains, w_qkv, w_out, out,
    xin, st_out, st_in, mod_in, mods, hid, wq, wo, own, chain, probs_ref, at, run, pp, sib, xo, xi, zo, zi,
    wq_sem, wo_sem,
    az_s, az_r, sz_s, sz_r, mz_s, mz_r, bx_s, bx_r, bc_s, bc_r, sx_s, sx_r, cc_s, cc_r,
    ch_s, ch_r, at_s, at_r, pc_s, pc_r, px_s, px_r, pz_s, pz_r,
):
    nt, ns, nm, tok, db, heads_cols, pc, nw = cfg
    tokh = tok // nm
    seq_len = tok * ns
    half = nt // 2
    groups = heads_cols // pc
    pieces = 3 * groups
    chunks = db // nw
    t, s, m = lax.axis_index("tm"), lax.axis_index("seq"), lax.axis_index("mp")
    om = 1 - m
    width = db * nt

    for j in range(groups):
        for c in range(3):
            pltpu.make_async_copy(
                w_qkv.at[c, :, pl.ds(j * pc, pc)], wq.at[j * 3 + c], wq_sem.at[j * 3 + c]
            ).start()
    for n in range(chunks):
        for j in range(groups):
            pltpu.make_async_copy(
                w_out.at[pl.ds(n * nw, nw), pl.ds(j * pc, pc)], wo.at[n, j], wo_sem.at[n, j]
            ).start()

    barrier = pltpu.get_barrier_semaphore()

    def greet(**where):
        pl.semaphore_signal(barrier, inc=1, device_id=where, device_id_type=MESH)

    for k in range(1, nt):
        greet(tm=lax.rem(t + k, nt), mp=m)
    for k in range(nt):
        greet(tm=lax.rem(t + k, nt), mp=om)
    for k in range(1, ns):
        greet(seq=lax.rem(s + k, ns))
    pl.semaphore_wait(barrier, 2 * nt - 1 + ns - 1)

    zs = [lax.rem(t + k, nt) for k in range(nt)]
    xs = [lax.rem(s + k, ns) for k in range(ns)]

    def az(k):
        return remote(xb.at[zs[k], m], xin.at[t, s, m], az_s.at[k], az_r.at[t], tm=zs[k])

    def sz(k):
        return remote(st_out, st_in.at[t, s], sz_s.at[k], sz_r.at[t], tm=zs[k])

    def mz(k):
        return remote(modp.at[zs[k]], mod_in.at[t], mz_s.at[k], mz_r.at[t], tm=zs[k])

    for k in range(1, nt):
        az(k).start()
    for k in range(1, nt):
        mz(k).start()
    xin[t, s] = xb[t]
    mod_in[t] = modp[t]

    def bx(tt, k):
        ref = xin.at[tt, s, m]
        return remote(ref, ref, bx_s.at[tt, k], bx_r.at[tt, s], seq=xs[k])

    def bc(tt):
        ref = xin.at[tt, s, m]
        return remote(ref, ref, bc_s.at[tt], bc_r.at[tt], mp=om)

    def sx(tt, k):
        ref = st_in.at[tt, s]
        return remote(ref, ref, sx_s.at[tt, k], sx_r.at[tt, s], seq=xs[k])

    def cc(tt, k):
        ref = xin.at[tt, xs[k], m]
        return remote(ref, ref, cc_s.at[tt, k], cc_r.at[tt, xs[k]], mp=om)

    for k in range(1, ns):
        bx(t, k).start()

    total = jnp.zeros((tok, 1), F32)
    for b in range(nt):
        total += jnp.sum(xb[b].reshape(tok, db).astype(F32), axis=-1, keepdims=True)
    mean = total / width
    total = jnp.zeros((tok, 1), F32)
    for b in range(nt):
        centred = xb[b].reshape(tok, db).astype(F32) - mean
        total += jnp.sum(centred * centred, axis=-1, keepdims=True)
    rstd = lax.rsqrt(total / width + norm_eps)
    lane = lax.broadcasted_iota(jnp.int32, (tok, 128), 1)
    both = jnp.where(lane == 0, mean, jnp.where(lane == 1, rstd, 0.0))
    if tok < 128:
        both = jnp.concatenate([both, jnp.zeros((128 - tok, 128), F32)], axis=0)
    st_out[...] = both.T[:8, :]
    st_in[t, s] = st_out[...]
    for k in range(1, nt):
        sz(k).start()
    for k in range(1, ns):
        sx(t, k).start()

    for k in range(1, nt):
        tt = zs[k]
        ref = xin.at[tt, s, m]
        remote(ref, ref, az_s.at[k], az_r.at[tt], tm=tt).wait_recv()
        for i in range(1, ns):
            bx(tt, i).start()
        bc(tt).start()
    for k in range(1, nt):
        tt = zs[k]
        ref = st_in.at[tt, s]
        remote(ref, ref, sz_s.at[k], sz_r.at[tt], tm=tt).wait_recv()
        for i in range(1, ns):
            sx(tt, i).start()
    for k in range(nt):
        tt = zs[k]
        for i in range(1, ns):
            ref = xin.at[tt, xs[i], m]
            remote(ref, ref, bx_s.at[tt, i], bx_r.at[tt, xs[i]], seq=xs[i]).wait_recv()
            cc(tt, i).start()

    for k in range(1, nt):
        tt = zs[k]
        ref = mod_in.at[tt]
        remote(ref, ref, mz_s.at[k], mz_r.at[tt], tm=tt).wait_recv()
    total = mod_in[0]
    for b in range(1, nt):
        total = total + mod_in[b]
    mods[...] = total

    def modulate(tt, carry):
        shift = mods[0, pl.ds(tt, 1), :]
        scale = mods[1, pl.ds(tt, 1), :]
        for ss in range(ns):
            stats = st_in[tt, ss].T
            x = xin[tt, ss].reshape(tok, db).astype(F32)
            normed = (x - stats[:tok, 0:1]) * stats[:tok, 1:2]
            hid[tt, pl.ds(ss * tok, tok), :] = (normed * (1.0 + scale) + shift).astype(BF16)
        return carry

    for k in range(nt):
        tt = zs[k]
        if k > 0:
            ref = xin.at[tt, s, om]
            remote(ref, ref, bc_s.at[tt], bc_r.at[tt], mp=om).wait_recv()
        for i in range(1, ns):
            ref = xin.at[tt, xs[i], om]
            remote(ref, ref, cc_s.at[tt, i], cc_r.at[tt, xs[i]], mp=om).wait_recv()
            ref = st_in.at[tt, xs[i]]
            remote(ref, ref, sx_s.at[tt, i], sx_r.at[tt, xs[i]], seq=xs[i]).wait_recv()
        modulate(tt, 0)

    def ch(p, d, h):
        ref = chain.at[p, d, h]
        dest = jnp.minimum(t + 1, nt - 1) if d == 1 else jnp.maximum(t - 1, 0)
        return remote(ref, ref, ch_s.at[p, d, h], ch_r.at[p, d, h], tm=dest)

    per = max(1, min(half, 256 // seq_len))

    def project(p, carry):
        pltpu.make_async_copy(w_qkv.at[0, :, pl.ds(0, pc)], wq.at[p], wq_sem.at[p]).wait()
        for d in range(2):
            is_first = t == (0 if d == 1 else nt - 1)

            def rows(g, c2):
                lhs = hid[pl.ds(d * half + g * per, per)].reshape(per * seq_len, db)
                prod = jnp.dot(lhs, wq[p], preferred_element_type=F32)
                prod = prod.reshape(per, seq_len, pc)
                own[p, d, pl.ds(g * per, per)] = prod

                @pl.when(is_first)
                def _():
                    chain[p, d, pl.ds(g * per, per)] = prod.astype(BF16)
                    for h in range(per):
                        ch(p, d, g * per + h).start()

                return c2

            lax.fori_loop(0, half // per, rows, 0)

        return carry


    inv_root = 1.0 / jnp.sqrt(F32(HEAD_DIM))

    def at_copy(j, d, h):
        ref = at.at[d, j, h]
        dest = jnp.maximum(t - 1, 0) if d == 1 else jnp.minimum(t + 1, nt - 1)
        return remote(ref, ref, at_s.at[d, j, h], at_r.at[d, j, h], tm=dest)

    def find_probs(j, d, h):
        for i in range(pc // HEAD_DIM):
            cols = slice(i * HEAD_DIM, (i + 1) * HEAD_DIM)

            def normed(which):
                v = own[3 * j + which, d, h, :, cols]
                meansq = jnp.mean(v * v, axis=-1, keepdims=True)
                first = pl.multiple_of(j * pc + i * HEAD_DIM, HEAD_DIM)
                g = gains[which:which + 1, pl.ds(first, HEAD_DIM)]
                return (v * lax.rsqrt(meansq + norm_eps) * g).astype(BF16)

            scores = lax.dot_general(
                normed(0), normed(1), (((1,), (1,)), ((), ())), preferred_element_type=F32
            ) * inv_root
            expo = jnp.exp(scores)
            probs_ref[h, i] = (expo / jnp.sum(expo, axis=-1, keepdims=True)).astype(BF16)

    def attend(j, d, h):
        for i in range(pc // HEAD_DIM):
            cols = slice(i * HEAD_DIM, (i + 1) * HEAD_DIM)
            v = own[3 * j + 2, d, h, :, cols].astype(BF16)
            at[d, j, h, :, cols] = jnp.dot(
                probs_ref[h, i], v, preferred_element_type=F32
            ).astype(BF16)

    steps = pieces * half
    skew, slack = 5, 4

    def chain_step(k, carry):
        @pl.when(k < pieces)
        def _():
            project(k, 0)

        for d in range(2):
            lag = skew * (t - 1 if d == 1 else nt - 2 - t)
            i = k - lag
            last = t == (nt - 1 if d == 1 else 0)

            @pl.when((lag >= 0) & (i >= 0) & (i < steps))
            def _():
                p, h = i // half, lax.rem(i, half)
                ref = chain.at[p, d, h]
                remote(ref, ref, ch_s.at[p, d, h], ch_r.at[p, d, h], mp=om).wait_recv()

                @pl.when(jnp.logical_not(last))
                def _():
                    chain[p, d, h] = (chain[p, d, h].astype(F32) + own[p, d, h]).astype(BF16)
                    ch(p, d, h).start()

                @pl.when(last)
                def _():
                    own[p, d, h] = chain[p, d, h].astype(F32) + own[p, d, h]
                    which, j = lax.rem(p, 3), p // 3

                    @pl.when(which == 1)
                    def _():
                        find_probs(j, d, h)

                    @pl.when(which == 2)
                    def _():
                        attend(j, d, h)
                        at_copy(j, d, h).start()

        for d in range(2):
            behind = nt - 1 - t if d == 1 else t
            i = k - skew * (nt - 2) - slack * behind
            p, h = jnp.maximum(i, 0) // half, lax.rem(jnp.maximum(i, 0), half)

            @pl.when((behind > 0) & (i >= 0) & (i < steps) & (lax.rem(p, 3) == 2))
            def _():
                j = p // 3
                ref = at.at[d, j, h]
                remote(ref, ref, at_s.at[d, j, h], at_r.at[d, j, h], mp=om).wait_recv()

                @pl.when(behind < nt - 1)
                def _():
                    at_copy(j, d, h).start()

        return carry

    lax.fori_loop(0, steps + skew * (nt - 2) + slack * (nt - 1), chain_step, 0)

    def pcopy(n):
        return remote(pp.at[n, om], sib.at[n], pc_s.at[n], pc_r.at[n], mp=om)

    def px(n, k):
        return remote(xo.at[n, xs[k]], xi.at[n, s], px_s.at[n, k], px_r.at[n, s], seq=xs[k])

    blocks = nt // nm
    om_t = t // blocks
    blk = lax.rem(t, blocks)

    def pz(n, tt):
        return remote(
            zo.at[n, tt], zi.at[n, blk, m], pz_s.at[n, tt], pz_r.at[n, blk, m], tm=tt, mp=om_t
        )

    def produce(n):
        for j in range(groups):
            pltpu.make_async_copy(
                w_out.at[pl.ds(n * nw, nw), pl.ds(j * pc, pc)], wo.at[n, j], wo_sem.at[n, j]
            ).wait()
        run[...] = jnp.zeros_like(run)
        for d in range(2):
            def one_step(h, carry):
                tt = d * half + h
                acc = jnp.zeros((seq_len, nw), F32)
                for j in range(groups):
                    acc += lax.dot_general(
                        at[d, j, h], wo[n, j], (((1,), (1,)), ((), ())), preferred_element_type=F32
                    )
                gate = mods[2, pl.ds(tt, 1), n * nw:(n + 1) * nw]
                gate = gate * dtb[pl.ds(tt, 1), n * nw:(n + 1) * nw]
                new = run[...] + gate * acc
                run[...] = new
                parted = new.reshape(ns, nm, tokh, nw)
                for hh in range(nm):
                    pp[n, hh, tt] = parted[:, hh]
                return carry

            lax.fori_loop(0, half, one_step, 0)
        pcopy(n).start()

    def fold(n):
        pcopy(n).wait_recv()

        def add(tt, carry):
            both = pp[n, m, tt] + sib[n, tt]
            pp[n, m, tt] = both
            for ss in range(ns):
                xo[n, ss, tt] = both[ss].astype(BF16)
            return carry

        lax.fori_loop(0, nt, add, 0)
        for k in range(1, ns):
            px(n, k).start()

    def to_owner(n, tt, act):
        @pl.when(jnp.logical_not((tt == t) & (om_t == m)))
        def _():
            act(pz(n, tt))

    def deliver(n):
        for k in range(1, ns):
            ref = xi.at[n, xs[k]]
            remote(ref, ref, px_s.at[n, k], px_r.at[n, xs[k]], seq=xs[k]).wait_recv()

        def finish(tt, carry):
            whole = pp[n, m, tt, s]
            for k in range(1, ns):
                whole = whole + xi[n, xs[k], tt].astype(F32)
            zo[n, tt] = whole
            to_owner(n, tt, lambda c: c.start())
            return carry

        lax.fori_loop(0, nt, finish, 0)

    for n in range(chunks + 2):
        if n < chunks:
            produce(n)
        if 0 <= n - 1 < chunks:
            fold(n - 1)
        if 0 <= n - 2 < chunks:
            deliver(n - 2)

    @pl.when(om_t == m)
    def _():
        for n in range(chunks):
            zi[n, blk, m] = zo[n, t]

    for n in range(chunks):
        for b in range(blocks):
            for mm in range(nm):
                here = (m * blocks + b == t) & (m == mm)
                ref = zi.at[n, b, mm]

                @pl.when(jnp.logical_not(here))
                def _():
                    remote(ref, ref, pz_s.at[n, 0], pz_r.at[n, b, mm], mp=om).wait_recv()

                out[mm * tokh:(mm + 1) * tokh, b * db + n * nw:b * db + (n + 1) * nw] = zi[n, b, mm]

    for k in range(1, nt):
        az(k).wait_send()
        mz(k).wait_send()
        sz(k).wait_send()
        bc(zs[k]).wait_send()
    for k in range(nt):
        for i in range(1, ns):
            bx(zs[k], i).wait_send()
            sx(zs[k], i).wait_send()
            cc(zs[k], i).wait_send()
    for d in range(2):
        last = t == (nt - 1 if d == 1 else 0)
        far = t == (0 if d == 1 else nt - 1)

        @pl.when(jnp.logical_not(last))
        def _():
            def body(p, carry):
                for h in range(half):
                    ch(p, d, h).wait_send()
                return carry

            lax.fori_loop(0, pieces, body, 0)

        @pl.when(jnp.logical_not(far))
        def _():
            def body(j, carry):
                for h in range(half):
                    at_copy(j, d, h).wait_send()
                return carry

            lax.fori_loop(0, groups, body, 0)
    for n in range(chunks):
        pcopy(n).wait_send()
        for k in range(1, ns):
            px(n, k).wait_send()

        def body(tt, carry):
            to_owner(n, tt, lambda c: c.wait_send())
            return carry

        lax.fori_loop(0, nt, body, 0)


def on_device(states, start_step, w_qkv, qk_gain, w_out, time_proj):
    _, tok, width = states.shape
    nt = lax.axis_size("tm")
    ns = lax.axis_size("seq")
    nm = lax.axis_size("mp")
    tm_pos = lax.axis_index("tm")
    db = width // nt
    heads_cols = w_qkv.shape[2]
    pc = 256 if heads_cols % 256 == 0 else heads_cols
    nw = 256 if db % 256 == 0 else db
    tokh = tok // nm
    seq_len = tok * ns
    half = nt // 2
    groups = heads_cols // pc
    pieces = 3 * groups
    chunks = db // nw
    blocks = nt // nm

    steps_idx = start_step[0] + jnp.arange(nt)
    sigma_now = sigma_of(steps_idx)
    step_size = sigma_of(steps_idx + 1) - sigma_now
    emb = embed_time(sigma_now)
    freq_rows = time_proj.shape[0]
    emb_cols = lax.dynamic_slice_in_dim(emb, tm_pos * freq_rows, freq_rows, 1)
    modp = jnp.dot(emb_cols, time_proj, preferred_element_type=F32)
    modp = modp.reshape(nt, 3, nt, db).transpose(2, 1, 0, 3)
    dtb = jnp.broadcast_to(step_size[:, None], (nt, db))
    xb = states.reshape(nm, tokh, nt, db).transpose(2, 0, 1, 3)

    dma = pltpu.SemaphoreType.DMA
    vmem = pltpu.VMEM
    cfg = (nt, ns, nm, tok, db, heads_cols, pc, nw)
    result = pl.pallas_call(
        functools.partial(sweep_kernel, cfg),
        out_shape=jax.ShapeDtypeStruct((tok, blocks * db), F32),
        in_specs=[pl.BlockSpec(memory_space=pltpu.VMEM)] * 4
        + [pl.BlockSpec(memory_space=pl.ANY)] * 2,
        out_specs=pl.BlockSpec(memory_space=pltpu.VMEM),
        scratch_shapes=[
            vmem((nt, ns, nm, tokh, db), BF16),
            vmem((8, 128), F32),
            vmem((nt, ns, 8, 128), F32),
            vmem((nt, 3, nt, db), F32),
            vmem((3, nt, db), F32),
            vmem((nt, seq_len, db), BF16),
            vmem((pieces, db, pc), BF16),
            vmem((chunks, groups, nw, pc), BF16),
            vmem((pieces, 2, half, seq_len, pc), F32),
            vmem((pieces, 2, half, seq_len, pc), BF16),
            vmem((half, pc // HEAD_DIM, seq_len, seq_len), BF16),
            vmem((2, groups, half, seq_len, pc), BF16),
            vmem((seq_len, nw), F32),
            vmem((chunks, nm, nt, ns, tokh, nw), F32),
            vmem((chunks, nt, ns, tokh, nw), F32),
            vmem((chunks, ns, nt, tokh, nw), BF16),
            vmem((chunks, ns, nt, tokh, nw), BF16),
            vmem((chunks, nt, tokh, nw), F32),
            vmem((chunks, blocks, nm, tokh, nw), F32),
            dma((pieces,)),
            dma((chunks, groups)),
            dma((nt,)), dma((nt,)),
            dma((nt,)), dma((nt,)),
            dma((nt,)), dma((nt,)),
            dma((nt, ns)), dma((nt, ns)),
            dma((nt,)), dma((nt,)),
            dma((nt, ns)), dma((nt, ns)),
            dma((nt, ns)), dma((nt, ns)),
            dma((pieces, 2, half)), dma((pieces, 2, half)),
            dma((2, groups, half)), dma((2, groups, half)),
            dma((chunks,)), dma((chunks,)),
            dma((chunks, ns)), dma((chunks, ns)),
            dma((chunks, nt)), dma((chunks, blocks, nm)),
        ],
        compiler_params=pltpu.CompilerParams(
            collective_id=0, has_side_effects=True, vmem_limit_bytes=60 * 1024 * 1024
        ),
    )(xb, modp, dtb, qk_gain, w_qkv, w_out)
    return result.reshape(1, tok, blocks * db)


def solution(mesh):
    return jax.shard_map(
        on_device,
        mesh=mesh,
        in_specs=(
            P(("group", "tm"), "seq", None),
            P("group"),
            P(None, "tm", ("seq", "mp")),
            P(None, ("seq", "mp")),
            P("tm", ("seq", "mp")),
            P("tm", None),
        ),
        out_specs=P(("group", "tm"), "seq", "mp"),
        check_vma=False,
    )
```
